512 devices in a mesh: ex: 32 (over z, core), feat: 16 (over y, x).
Axes of the slice: x: 4, y: 4, z: 16, core: 2. Of those that a mesh axis runs over, the one named last changes fastest.
Arguments:
- features: bfloat16 [65536, 16384], P('ex', 'feat'), may hold values from -24 to 24
- test_matrix: bfloat16 [16384, 128], P('feat'), may hold values from -0.046875 to 0.046875
Outputs:
- first_range: float32 [65536, 128], P('ex')
- basis: float32 [65536, 128], P('ex')
- projected: float32 [128, 16384], P(None, 'feat')
The draws below stay inside these ranges and needn't reach their ends.
All inputs are finite; a program needn't handle non-finite values.
Results may differ from the reference program's by a relative error of at most 0.0028.
Values sent between devices are 32-bit elements; how exact they have to be, the bound alone decides.
A program may use at most 64 MiB of HBM per device.

```python
import jax
import jax.numpy as jnp
from jax import lax

DIMS = 16384
RANK = 128
ROWS = 65536


def draw_features(key, part):
    key = jax.random.fold_in(key, 11)
    row_pos = jnp.arange(ROWS, dtype=jnp.float32)[:, None] / jnp.float32(ROWS)
    base = jnp.clip(jax.random.normal(key, (ROWS, DIMS), jnp.float32), -6.0, 6.0)
    spread = jnp.log(jnp.float32(4.0))
    return (base * jnp.exp(spread * row_pos)).astype(jnp.bfloat16)


def steps_of(rng, shape, pieces, least, high):
    gain = 1.0
    for dim, blocks in pieces:
        steps = jax.random.uniform(jax.random.fold_in(jax.random.fold_in(rng, 6), dim), (blocks,), jnp.float32, least / len(pieces), high / len(pieces))
        gain = gain * jnp.repeat(jnp.exp(steps), shape[dim] // blocks).reshape((-1,) + (1,) * (len(shape) - 1 - dim))
    return gain


def noise(key, dims, scale, most, pieces=(), held_as=jnp.bfloat16):
    level = steps_of(key, dims, pieces, -0.22, 0.18) if pieces else 1.0
    entries = jax.random.normal(key, dims, jnp.float32) * scale * level
    return jnp.minimum(jnp.maximum(entries, -most), most).astype(held_as)


def setup_inputs(seed: int = 0) -> dict:
    key_of = jax.random.split(jax.random.key(seed), 3)
    return {
        "features": draw_features(jax.random.fold_in(key_of[2], 71), 0),
        "test_matrix": noise(key_of[1], (DIMS, RANK), DIMS ** -0.5, 0.046875, ((0, 16),)),
    }


def orthonormalize(sketch):
    gram = jnp.dot(sketch.T.astype(jnp.float32), sketch.astype(jnp.float32), preferred_element_type=jnp.float32, precision=lax.Precision.HIGHEST)
    lower = jnp.linalg.cholesky(gram)
    return jax.scipy.linalg.solve_triangular(lower, sketch.T, lower=True).T

def reference(features, test_matrix):
    scale = jnp.sqrt(jnp.float32(ROWS))
    shrink = 1.0 / jnp.sqrt(jnp.float32(DIMS))
    sketch = jnp.dot(features.astype(jnp.float32), test_matrix.astype(jnp.float32), preferred_element_type=jnp.float32)
    first_ortho = orthonormalize(sketch)
    first_range = first_ortho * scale
    first_basis = first_ortho.astype(jnp.bfloat16)
    power_sum = jnp.dot(features.T.astype(jnp.float32), first_basis.astype(jnp.float32), preferred_element_type=jnp.float32)
    power = (power_sum * shrink).astype(jnp.bfloat16)
    second = jnp.dot(features.astype(jnp.float32), power.astype(jnp.float32), preferred_element_type=jnp.float32)
    ortho = orthonormalize(second)
    basis = ortho * scale
    projected = jnp.dot(ortho.astype(jnp.bfloat16).T.astype(jnp.float32), features.astype(jnp.float32), preferred_element_type=jnp.float32)
    return (first_range, basis, projected)
```

```python
import functools

import jax
import jax.numpy as jnp
from jax import lax
from jax.experimental import pallas as pl
from jax.experimental.pallas import tpu as pltpu
from jax.sharding import PartitionSpec as P

DIMS = 16384
ROWS = 65536
RANK = 128
MESH = pl.DeviceIdType.MESH
F32 = jnp.float32
BF16 = jnp.bfloat16
HIGHEST = lax.Precision.HIGHEST
BLOCK = 8


def split3(value):
    high = value.astype(BF16)
    rest = value - high.astype(F32)
    middle = rest.astype(BF16)
    low = (rest - middle.astype(F32)).astype(BF16)
    return high, middle, low


def factor(work):
    lane = lax.broadcasted_iota(jnp.int32, (BLOCK, RANK), 1)

    def step(b, carry):
        at = pl.ds(pl.multiple_of(b * BLOCK, BLOCK), BLOCK)
        left = work[at, 0:RANK]
        right = work[at, RANK : 2 * RANK]
        diag = {}
        for j in range(BLOCK):
            column = jnp.sum(jnp.where(lane == b * BLOCK + j, left, 0.0), axis=1, keepdims=True)
            column = jnp.broadcast_to(column, (BLOCK, RANK))
            for i in range(j, BLOCK):
                diag[i, j] = column[i : i + 1, :]
        lrows = [left[i : i + 1, :] for i in range(BLOCK)]
        rrows = [right[i : i + 1, :] for i in range(BLOCK)]
        for j in range(BLOCK):
            inv = lax.rsqrt(diag[j, j])
            lrows[j] = lrows[j] * inv
            rrows[j] = rrows[j] * inv
            low = {i: diag[i, j] * inv for i in range(j + 1, BLOCK)}
            for i in range(j + 1, BLOCK):
                for k in range(j + 1, i + 1):
                    diag[i, k] = diag[i, k] - low[i] * low[k]
                lrows[i] = lrows[i] - low[i] * lrows[j]
                rrows[i] = rrows[i] - low[i] * rrows[j]
        left = jnp.concatenate(lrows, axis=0)
        right = jnp.concatenate(rrows, axis=0)
        below = jnp.where(lane >= (b + 1) * BLOCK, left, 0.0)
        both = jnp.concatenate([left, right], axis=1)
        work[...] -= lax.dot_general(
            below, both, (((0,), (0,)), ((), ())), preferred_element_type=F32, precision=HIGHEST
        )
        work[at, 0:RANK] = left
        work[at, RANK : 2 * RANK] = right
        return carry

    lax.fori_loop(0, RANK // BLOCK, step, 0)


class Grid:
    def __init__(self, nx, ny, nz):
        self.nx, self.ny, self.nz = nx, ny, nz
        ex, feat = lax.axis_index("ex"), lax.axis_index("feat")
        self.ex, self.feat = ex, feat
        self.x, self.y = lax.rem(feat, nx), lax.div(feat, nx)
        self.core, self.z = lax.rem(ex, 2), lax.div(ex, 2)

    def xpeer(self, k):
        to = lax.rem(self.x + k, self.nx)
        return to, (self.ex, self.y * self.nx + to)

    def ypeer(self, k):
        to = lax.rem(self.y + k, self.ny)
        return to, (self.ex, to * self.nx + self.x)

    def zpeer(self, k):
        to = lax.rem(self.z + k, self.nz)
        return to, (to * 2 + self.core, self.feat)

    def sibling(self):
        return (self.z * 2 + 1 - self.core, self.feat)

    def peers(self):
        out = [self.xpeer(k)[1] for k in range(1, self.nx)]
        out += [self.ypeer(k)[1] for k in range(1, self.ny)]
        return out + [self.sibling()]


def remote(src, dst, send, recv, to):
    return pltpu.make_async_remote_copy(
        src_ref=src, dst_ref=dst, send_sem=send, recv_sem=recv, device_id=to, device_id_type=MESH
    )


class FeatSum:
    SCRATCH = 12

    @staticmethod
    def scratch(nx, ny, rows):
        r, h = RANK // (nx * ny), rows // 2
        sems = [pltpu.SemaphoreType.DMA((4, nx - 1)), pltpu.SemaphoreType.DMA((4, nx - 1))]
        sems += [pltpu.SemaphoreType.DMA((4, ny - 1)), pltpu.SemaphoreType.DMA((4, ny - 1))]
        return [
            pltpu.VMEM((ny, nx, r, rows), F32),
            pltpu.VMEM((ny, nx, r, rows), F32),
            pltpu.VMEM((nx - 1, ny, r, h), F32),
            pltpu.VMEM((ny - 1, nx, r, h), F32),
            pltpu.VMEM((ny, r, h), F32),
            pltpu.VMEM((nx, r, h), F32),
            pltpu.VMEM((ny - 1, r, h), F32),
            pltpu.VMEM((nx - 1, r, h), F32),
        ] + sems

    def __init__(self, grid, refs):
        self.g = grid
        (self.part, self.full, self.r1a, self.r1b, self.s1a, self.s1b, self.r2a, self.r2b,
         self.xs, self.xr, self.ys, self.yr) = refs
        rows = self.part.shape[3]
        self.a, self.b = pl.ds(0, rows // 2), pl.ds(rows // 2, rows // 2)

    def over_x(self, n, src, dst):
        out = []
        for k in range(1, self.g.nx):
            to, device = self.g.xpeer(k)
            out.append(remote(src(to), dst(k - 1), self.xs.at[n, k - 1], self.xr.at[n, k - 1], device))
            out[-1].start()
        return out

    def over_y(self, n, src, dst):
        out = []
        for k in range(1, self.g.ny):
            to, device = self.g.ypeer(k)
            out.append(remote(src(to), dst(k - 1), self.ys.at[n, k - 1], self.yr.at[n, k - 1], device))
            out[-1].start()
        return out

    def start_a(self):
        self.c1a = self.over_x(0, lambda to: self.part.at[:, to, :, self.a], lambda k: self.r1a.at[k])

    def start_b(self):
        self.c1b = self.over_y(0, lambda to: self.part.at[to, :, :, self.b], lambda k: self.r1b.at[k])

    def finish(self):
        x, y = self.g.x, self.g.y
        full = self.full
        for c in self.c1a:
            c.wait_recv()
        self.s1a[...] = self.part[:, x, :, self.a] + sum(self.r1a[k] for k in range(self.g.nx - 1))
        c2a = self.over_y(1, lambda to: self.s1a.at[to], lambda k: self.r2a.at[k])
        for c in self.c1b:
            c.wait_recv()
        self.s1b[...] = self.part[y, :, :, self.b] + sum(self.r1b[k] for k in range(self.g.ny - 1))
        c2b = self.over_x(1, lambda to: self.s1b.at[to], lambda k: self.r2b.at[k])
        for c in c2a:
            c.wait_recv()
        full[y, x, :, self.a] = self.s1a[y] + sum(self.r2a[k] for k in range(self.g.ny - 1))
        own_a, own_b = full.at[y, x, :, self.a], full.at[y, x, :, self.b]
        c3a = self.over_y(2, lambda to: own_a, lambda k: own_a)
        for c in c2b:
            c.wait_recv()
        full[y, x, :, self.b] = self.s1b[x] + sum(self.r2b[k] for k in range(self.g.nx - 1))
        c3b = self.over_x(2, lambda to: own_b, lambda k: own_b)
        for c in c3a:
            c.wait_recv()
        col_a, row_b = full.at[:, x, :, self.a], full.at[y, :, :, self.b]
        c4a = self.over_x(3, lambda to: col_a, lambda k: col_a)
        for c in c3b:
            c.wait_recv()
        c4b = self.over_y(3, lambda to: row_b, lambda k: row_b)
        for c in c4a + c4b:
            c.wait_recv()
        self.sent = self.c1a + self.c1b + c2a + c2b + c3a + c3b + c4a + c4b

    def drain(self):
        for c in self.sent:
            c.wait_send()


class GramSum:
    SCRATCH = 9

    @staticmethod
    def scratch(nx, ny, nz):
        r = RANK // (nx * ny)
        return [
            pltpu.VMEM((r, RANK), F32),
            pltpu.VMEM((r, RANK), F32),
            pltpu.VMEM((r, RANK), F32),
            pltpu.VMEM((nz - 1, r, RANK), F32),
            pltpu.VMEM((ny, nx, r, RANK), F32),
            pltpu.SemaphoreType.DMA((1 + nx - 1 + ny - 1,)),
            pltpu.SemaphoreType.DMA((1 + nx - 1 + ny - 1,)),
            pltpu.SemaphoreType.DMA((nz - 1,)),
            pltpu.SemaphoreType.DMA((nz - 1,)),
        ]

    def __init__(self, grid, refs):
        self.g = grid
        (self.own, self.rc, self.pair, self.rz, self.full, self.ss, self.rs, self.zs, self.zr) = refs

    def start(self):
        self.c0 = remote(self.own, self.rc, self.ss.at[0], self.rs.at[0], self.g.sibling())
        self.c0.start()

    def zcopy(self, k):
        _, device = self.g.zpeer(k)
        return remote(self.pair, self.rz.at[k - 1], self.zs.at[k - 1], self.zr.at[k - 1], device)

    def over_z(self):
        self.c0.wait_recv()
        self.pair[...] = self.own[...] + self.rc[...]

        def go(k, carry):
            self.zcopy(k).start()
            return carry

        lax.fori_loop(1, self.g.nz, go, 0)

    def finish(self):
        g = self.g

        def wait(k, carry):
            self.zcopy(k).wait_recv()
            return carry

        lax.fori_loop(1, g.nz, wait, 0)
        self.full[g.y, g.x] = self.pair[...] + jnp.sum(self.rz[...], axis=0)
        own = self.full.at[g.y, g.x]
        cx = []
        for k in range(1, g.nx):
            cx.append(remote(own, own, self.ss.at[k], self.rs.at[k], g.xpeer(k)[1]))
            cx[-1].start()
        for c in cx:
            c.wait_recv()
        row = self.full.at[g.y]
        cy = []
        for k in range(1, g.ny):
            n = g.nx - 1 + k
            cy.append(remote(row, row, self.ss.at[n], self.rs.at[n], g.ypeer(k)[1]))
            cy[-1].start()
        for c in cy:
            c.wait_recv()
        self.sent = [self.c0] + cx + cy
        return self.full[...].reshape(RANK, RANK)

    def drain(self):
        for c in self.sent:
            c.wait_send()

        def wait(k, carry):
            self.zcopy(k).wait_send()
            return carry

        lax.fori_loop(1, self.g.nz, wait, 0)


class ExSum:
    SCRATCH = 10

    @staticmethod
    def scratch(nz, dims):
        r, h = RANK // nz, dims // 2
        return [
            pltpu.VMEM((2, nz, r, h), F32),
            pltpu.VMEM((nz, r, h), F32),
            pltpu.VMEM((nz, r, h), F32),
            pltpu.VMEM((nz - 1, r, h), F32),
            pltpu.VMEM((2, nz, r, h), F32),
            pltpu.SemaphoreType.DMA((2,)),
            pltpu.SemaphoreType.DMA((2,)),
            pltpu.SemaphoreType.DMA((2, nz - 1)),
            pltpu.SemaphoreType.DMA((2, nz - 1)),
        ]

    def __init__(self, grid, refs):
        self.g = grid
        (self.part, self.rc, self.pair, self.rz, self.full, self.cs, self.cr, self.zs, self.zr) = refs

    def start(self):
        other = 1 - self.g.core
        self.c0 = remote(self.part.at[other], self.rc, self.cs.at[0], self.cr.at[0], self.g.sibling())
        self.c0.start()

    def scatter(self, k):
        to, device = self.g.zpeer(k)
        return remote(self.pair.at[to], self.rz.at[k - 1], self.zs.at[0, k - 1], self.zr.at[0, k - 1], device)

    def gather(self, k):
        own = self.full.at[self.g.core, self.g.z]
        return remote(own, own, self.zs.at[1, k - 1], self.zr.at[1, k - 1], self.g.zpeer(k)[1])

    def loop(self, act):
        def body(k, carry):
            act(k)
            return carry

        lax.fori_loop(1, self.g.nz, body, 0)

    def over_z(self):
        self.c0.wait_recv()
        self.pair[...] = self.part[self.g.core] + self.rc[...]
        self.loop(lambda k: self.scatter(k).start())

    def spread(self):
        g = self.g
        self.loop(lambda k: self.scatter(k).wait_recv())
        self.full[g.core, g.z] = self.pair[g.z] + jnp.sum(self.rz[...], axis=0)
        self.loop(lambda k: self.gather(k).start())

    def arrive(self):
        self.loop(lambda k: self.gather(k).wait_recv())
        half = self.full.at[self.g.core]
        self.c1 = remote(half, half, self.cs.at[1], self.cr.at[1], self.g.sibling())
        self.c1.start()

    def drain(self):
        self.c0.wait_send()
        self.c1.wait_send()
        self.loop(lambda k: self.scatter(k).wait_send())
        self.loop(lambda k: self.gather(k).wait_send())


def kernel(nx, ny, nz, a_hbm, t_ref, first_hbm, basis_hbm, proj_hbm, a_ref, work, inv_ref, rows_ref, proj_ref,
           power_ref, a_sem, out_sem, *refs):
    g = Grid(nx, ny, nz)
    rows, dims = a_ref.shape
    refs = list(refs)

    def take(kind, n):
        out = kind(g, refs[:n])
        del refs[:n]
        return out

    sums = []
    for _ in range(2):
        sums.append((take(FeatSum, 12), take(GramSum, 9), take(ExSum, 9)))

    quarter = rows // 4
    loads = []
    for q in range(4):
        at = pl.ds(q * quarter, quarter)
        loads.append(pltpu.make_async_copy(a_hbm.at[at], a_ref.at[at], a_sem.at[q]))
        loads[-1].start()

    barrier = pltpu.get_barrier_semaphore()
    for device in g.peers():
        pl.semaphore_signal(barrier, inc=1, device_id=device, device_id_type=MESH)

    def greet(k, carry):
        pl.semaphore_signal(barrier, inc=1, device_id=g.zpeer(k)[1], device_id_type=MESH)
        return carry

    lax.fori_loop(1, nz, greet, 0)

    scale = jnp.sqrt(jnp.float32(ROWS))
    shrink = 1.0 / jnp.sqrt(jnp.float32(DIMS))
    shape = (ny, nx, RANK // (nx * ny), quarter)

    def round_trip(feat_sum, gram_sum, ex_sum):
        def rows_at(q):
            return feat_sum.full[:, :, :, q * quarter : (q + 1) * quarter].reshape(RANK, quarter)

        own = jnp.zeros((RANK // (nx * ny), RANK), F32)
        for q in range(4):
            mine = feat_sum.full[g.y, g.x, :, q * quarter : (q + 1) * quarter]
            own += lax.dot_general(mine, rows_at(q), (((1,), (1,)), ((), ())),
                                   preferred_element_type=F32, precision=HIGHEST)
        gram_sum.own[...] = own
        gram_sum.start()
        for q in range(4):
            terms = split3(rows_at(q))
            for n, term in enumerate(terms):
                rows_ref[n * RANK : (n + 1) * RANK, q * quarter : (q + 1) * quarter] = term
        h = dims // 2
        for s in range(2):
            half = 1 - g.core if s == 0 else g.core
            at = pl.ds(pl.multiple_of(half * h, h), h)
            prod = jnp.dot(rows_ref[...], a_ref[:, at], preferred_element_type=F32)
            prod = prod[:RANK] + prod[RANK : 2 * RANK] + prod[2 * RANK :]
            ex_sum.part[half] = prod.reshape(nz, RANK // nz, h)
            if s == 0:
                ex_sum.start()
                gram_sum.over_z()
        ex_sum.over_z()
        gram = gram_sum.finish()
        row = lax.broadcasted_iota(jnp.int32, (RANK, RANK), 0)
        column = lax.broadcasted_iota(jnp.int32, (RANK, RANK), 1)
        work[:, 0:RANK] = gram
        work[:, RANK : 2 * RANK] = jnp.where(row == column, 1.0, 0.0).astype(F32)
        ex_sum.spread()
        factor(work)
        inv_ref[...] = work[:, RANK : 2 * RANK]

    def write_rows(feat_sum, out_ref):
        def body(q, carry):
            at = pl.ds(pl.multiple_of(q * RANK, RANK), RANK)
            block = feat_sum.full[:, :, :, at].reshape(RANK, RANK)
            block = jnp.dot(inv_ref[...], block, preferred_element_type=F32, precision=HIGHEST)
            out_ref[at, :] = block.T * scale
            return carry

        lax.fori_loop(0, rows // RANK, body, 0)

    first, gram, ex = sums[0]
    first_out, basis_out = feat_rows_out = (refs[0], refs[1])
    test = t_ref[...].astype(F32).T.astype(BF16)
    for q in range(4):
        loads[q].wait()
        at = slice(q * quarter, (q + 1) * quarter)
        prod = lax.dot_general(test, a_ref[at, :], (((1,), (1,)), ((), ())), preferred_element_type=F32)
        first.part[:, :, :, at] = prod.reshape(shape)
        if q == 1:
            pl.semaphore_wait(barrier, nx - 1 + ny - 1 + nz - 1 + 1)
            first.start_a()
        if q == 3:
            first.start_b()
    first.finish()
    round_trip(first, gram, ex)
    write_rows(first, first_out)
    out1 = pltpu.make_async_copy(first_out, first_hbm, out_sem.at[0])
    out1.start()
    ex.arrive()

    second, gram2, ex2 = sums[1]
    h = dims // 2

    def power_half(half):
        w = ex.full[half].reshape(RANK, h)
        w = jnp.dot(inv_ref[...], w, preferred_element_type=F32, precision=HIGHEST)
        power_ref[half] = (w * shrink).astype(BF16)

    power_half(g.core)
    ex.c1.wait_recv()
    power_half(1 - g.core)
    for q in range(4):
        at = slice(q * quarter, (q + 1) * quarter)
        prod = lax.dot_general(power_ref[0], a_ref[at, 0:h], (((1,), (1,)), ((), ())), preferred_element_type=F32)
        prod += lax.dot_general(power_ref[1], a_ref[at, h:dims], (((1,), (1,)), ((), ())), preferred_element_type=F32)
        second.part[:, :, :, at] = prod.reshape(shape)
        if q == 1:
            second.start_a()
        if q == 3:
            second.start_b()
    second.finish()
    round_trip(second, gram2, ex2)
    write_rows(second, basis_out)
    out2 = pltpu.make_async_copy(basis_out, basis_hbm, out_sem.at[1])
    out2.start()
    ex2.arrive()

    def project_half(half):
        w = ex2.full[half].reshape(RANK, h)
        at = pl.ds(pl.multiple_of(half * h, h), h)
        proj_ref[:, at] = jnp.dot(inv_ref[...], w, preferred_element_type=F32, precision=HIGHEST)

    project_half(g.core)
    ex2.c1.wait_recv()
    project_half(1 - g.core)
    out3 = pltpu.make_async_copy(proj_ref, proj_hbm, out_sem.at[2])
    out3.start()
    for group in sums:
        for one in group:
            one.drain()
    out1.wait()
    out2.wait()
    out3.wait()


def shards(nx, ny, nz, features, test_matrix):
    rows, dims = features.shape
    hbm = pl.BlockSpec(memory_space=pl.ANY)
    scratch = [
        pltpu.VMEM((rows, dims), BF16),
        pltpu.VMEM((RANK, 2 * RANK), F32),
        pltpu.VMEM((RANK, RANK), F32),
        pltpu.VMEM((3 * RANK, rows), BF16),
        pltpu.VMEM((RANK, dims), F32),
        pltpu.VMEM((2, RANK, dims // 2), BF16),
        pltpu.SemaphoreType.DMA((4,)),
        pltpu.SemaphoreType.DMA((3,)),
    ]
    for _ in range(2):
        scratch += FeatSum.scratch(nx, ny, rows) + GramSum.scratch(nx, ny, nz) + ExSum.scratch(nz, dims)
    scratch += [pltpu.VMEM((rows, RANK), F32)] * 2
    return pl.pallas_call(
        functools.partial(kernel, nx, ny, nz),
        out_shape=(
            jax.ShapeDtypeStruct((rows, RANK), F32),
            jax.ShapeDtypeStruct((rows, RANK), F32),
            jax.ShapeDtypeStruct((RANK, dims), F32),
        ),
        in_specs=[hbm, pl.BlockSpec(memory_space=pltpu.VMEM)],
        out_specs=(hbm, hbm, hbm),
        scratch_shapes=scratch,
        compiler_params=pltpu.CompilerParams(
            collective_id=0, has_side_effects=True, vmem_limit_bytes=48 * 1024 * 1024
        ),
        cost_estimate=pl.CostEstimate(flops=6 * rows * dims * RANK * 2, bytes_accessed=8 << 20, transcendentals=256),
    )(features, test_matrix)


def solution(mesh):
    feat, ex = mesh.shape["feat"], mesh.shape["ex"]
    nx = {16: 4, 4: 2}[feat]
    return jax.shard_map(
        functools.partial(shards, nx, feat // nx, ex // 2),
        mesh=mesh,
        in_specs=(P("ex", "feat"), P("feat", None)),
        out_specs=(P("ex", None), P("ex", None), P(None, "feat")),
        check_vma=False,
    )
```

```python
import functools

import jax
import jax.numpy as jnp
from jax import lax
from jax.experimental import pallas as pl
from jax.experimental.pallas import tpu as pltpu
from jax.sharding import PartitionSpec as P

DIMS = 16384
ROWS = 65536
RANK = 128
MESH = pl.DeviceIdType.MESH
F32 = jnp.float32
BF16 = jnp.bfloat16
HIGHEST = lax.Precision.HIGHEST
BLOCK = 8
CHUNKS = 2


def split(value):
    high = value.astype(BF16)
    return high, (value - high.astype(F32)).astype(BF16)


def factor(work, begin, end):
    lane = lax.broadcasted_iota(jnp.int32, (BLOCK, RANK), 1)

    def step(b, carry):
        at = pl.ds(pl.multiple_of(b * BLOCK, BLOCK), BLOCK)
        left = work[at, 0:RANK]
        right = work[at, RANK : 2 * RANK]
        diag = {}
        for j in range(BLOCK):
            column = jnp.sum(jnp.where(lane == b * BLOCK + j, left, 0.0), axis=1, keepdims=True)
            column = jnp.broadcast_to(column, (BLOCK, RANK))
            for i in range(j, BLOCK):
                diag[i, j] = column[i : i + 1, :]
        lrows = [left[i : i + 1, :] for i in range(BLOCK)]
        rrows = [right[i : i + 1, :] for i in range(BLOCK)]
        for j in range(BLOCK):
            inv = lax.rsqrt(diag[j, j])
            lrows[j] = lrows[j] * inv
            rrows[j] = rrows[j] * inv
            low = {i: diag[i, j] * inv for i in range(j + 1, BLOCK)}
            for i in range(j + 1, BLOCK):
                for k in range(j + 1, i + 1):
                    diag[i, k] = diag[i, k] - low[i] * low[k]
                lrows[i] = lrows[i] - low[i] * lrows[j]
                rrows[i] = rrows[i] - low[i] * rrows[j]
        left = jnp.concatenate(lrows, axis=0)
        right = jnp.concatenate(rrows, axis=0)
        below = jnp.where(lane >= (b + 1) * BLOCK, left, 0.0)
        both = jnp.concatenate([left, right], axis=1)
        work[...] -= lax.dot_general(
            below, both, (((0,), (0,)), ((), ())), preferred_element_type=F32, precision=HIGHEST
        )
        work[at, 0:RANK] = left
        work[at, RANK : 2 * RANK] = right
        return carry

    lax.fori_loop(begin, end, step, 0)


class Axis:
    def __init__(self, n, me, device):
        self.n, self.me, self.device = n, me, device

    def at(self, offset):
        return lax.rem(self.me + offset + self.n, self.n)

    def peer(self, offset):
        return self.device(self.at(offset))


class Grid:
    def __init__(self, nx, ny, nz):
        ex, feat = lax.axis_index("ex"), lax.axis_index("feat")
        x, y = lax.rem(feat, nx), lax.div(feat, nx)
        core, z = lax.rem(ex, 2), lax.div(ex, 2)
        self.core = core
        self.x = Axis(nx, x, lambda i: (ex, y * nx + i))
        self.y = Axis(ny, y, lambda i: (ex, i * nx + x))
        self.z = Axis(nz, z, lambda i: (i * 2 + core, feat))
        self.sibling = (z * 2 + 1 - core, feat)

    def greet(self):
        barrier = pltpu.get_barrier_semaphore()
        partners = [self.sibling]
        for axis in (self.x, self.y):
            partners += [axis.peer(k) for k in range(1, axis.n)]
        partners += [self.z.peer(k) for k in range(1, self.z.n)]
        for device in partners:
            pl.semaphore_signal(barrier, inc=1, device_id=device, device_id_type=MESH)
        return lambda: pl.semaphore_wait(barrier, len(partners))


class Copies:
    def __init__(self, send, recv):
        self.send_sem, self.recv_sem = send, recv
        self.started = []

    @staticmethod
    def scratch(n):
        return [pltpu.SemaphoreType.DMA((n,)), pltpu.SemaphoreType.DMA((n,))]

    def send(self, device, src, dst):
        n = len(self.started)
        copy = pltpu.make_async_remote_copy(
            src_ref=src, dst_ref=dst, send_sem=self.send_sem.at[n], recv_sem=self.recv_sem.at[n],
            device_id=device, device_id_type=MESH,
        )
        copy.start()
        self.started.append(copy)
        return copy

    def drain(self):
        for copy in self.started:
            copy.wait_send()


def far_first(axis, i):
    return lax.rem((2 * lax.rem(i, 2) - 1) * (axis.n // 2 - lax.div(i + 1, 2)) + axis.n, axis.n)


class Along:
    def __init__(self, axis, send, recv):
        self.axis, self.send_sem, self.recv_sem = axis, send, recv

    @staticmethod
    def scratch(n):
        return [pltpu.SemaphoreType.DMA((n - 1,)), pltpu.SemaphoreType.DMA((n - 1,))]

    def copy(self, i):
        to = self.axis.at(far_first(self.axis, i))
        return pltpu.make_async_remote_copy(
            src_ref=self.src(to), dst_ref=self.dst(i), send_sem=self.send_sem.at[i], recv_sem=self.recv_sem.at[i],
            device_id=self.axis.device(to), device_id_type=MESH,
        )

    def loop(self, act):
        def body(i, carry):
            act(self.copy(i))
            return carry

        if self.axis.n > 4:
            lax.fori_loop(0, self.axis.n - 1, body, 0)
        else:
            for i in range(self.axis.n - 1):
                body(i, 0)

    def start(self, src, dst):
        self.src, self.dst = src, dst
        self.loop(lambda copy: copy.start())

    def wait(self):
        self.loop(lambda copy: copy.wait_recv())

    def drain(self):
        self.loop(lambda copy: copy.wait_send())


class FeatSum:
    @staticmethod
    def scratch(nx, ny, ranks, rows):
        e, h = rows // (nx * ny), ranks // 2
        sems = []
        for _ in range(4):
            sems += Along.scratch(nx) + Along.scratch(ny)
        return [
            pltpu.VMEM((ny, nx, ranks, e), F32),
            pltpu.VMEM((ny, nx, ranks, e), F32),
            pltpu.VMEM((nx - 1, ny, h, e), F32),
            pltpu.VMEM((ny - 1, nx, h, e), F32),
            pltpu.VMEM((ny, h, e), F32),
            pltpu.VMEM((nx, h, e), F32),
            pltpu.VMEM((ny - 1, h, e), F32),
            pltpu.VMEM((nx - 1, h, e), F32),
        ] + sems

    def __init__(self, grid, refs):
        self.g = grid
        self.part, self.full, self.r1a, self.r1b, self.sa, self.sb, self.r2a, self.r2b = refs[:8]
        sems = refs[8:]
        self.ax = [Along(grid.x, *sems[4 * n : 4 * n + 2]) for n in range(4)]
        self.ay = [Along(grid.y, *sems[4 * n + 2 : 4 * n + 4]) for n in range(4)]

    def drain(self):
        for one in self.ax + self.ay:
            one.drain()

    def run(self):
        x, y = self.g.x, self.g.y
        part, full = self.part, self.full
        h = part.shape[2] // 2
        a, b = pl.ds(0, h), pl.ds(h, h)
        self.ax[0].start(lambda to: part.at[:, to, a], lambda i: self.r1a.at[i])
        self.ay[0].start(lambda to: part.at[to, :, b], lambda i: self.r1b.at[i])
        yield
        self.ax[0].wait()
        self.sa[...] = part[:, x.me, a] + sum(self.r1a[i] for i in range(x.n - 1))
        self.ay[1].start(lambda to: self.sa.at[to], lambda i: self.r2a.at[i])
        self.ay[0].wait()
        self.sb[...] = part[y.me, :, b] + sum(self.r1b[i] for i in range(y.n - 1))
        self.ax[1].start(lambda to: self.sb.at[to], lambda i: self.r2b.at[i])
        yield
        own_a, own_b = full.at[y.me, x.me, a], full.at[y.me, x.me, b]
        self.ay[1].wait()
        own_a[...] = self.sa[y.me] + sum(self.r2a[i] for i in range(y.n - 1))
        self.ay[2].start(lambda to: own_a, lambda i: own_a)
        self.ax[1].wait()
        own_b[...] = self.sb[x.me] + sum(self.r2b[i] for i in range(x.n - 1))
        self.ax[2].start(lambda to: own_b, lambda i: own_b)
        yield
        column_a, row_b = full.at[:, x.me, a], full.at[y.me, :, b]
        self.ay[2].wait()
        self.ax[3].start(lambda to: column_a, lambda i: column_a)
        self.ax[2].wait()
        self.ay[3].start(lambda to: row_b, lambda i: row_b)
        yield
        self.ax[3].wait()
        self.ay[3].wait()


class GramSum:
    @staticmethod
    def scratch(nx, ny, nz):
        r = RANK // (nx * ny)
        return [
            pltpu.VMEM((r, RANK), F32),
            pltpu.VMEM((r, RANK), F32),
            pltpu.VMEM((r, RANK), F32),
            pltpu.VMEM((nz - 1, r, RANK), F32),
            pltpu.VMEM((ny, nx, r, RANK), F32),
        ] + Copies.scratch(1) + Along.scratch(nz) + Along.scratch(nx) + Along.scratch(ny)

    def __init__(self, grid, refs):
        self.g = grid
        self.own, self.rc, self.pair, self.rz, self.full = refs[:5]
        self.copies = Copies(*refs[5:7])
        self.az, self.ax, self.ay = Along(grid.z, *refs[7:9]), Along(grid.x, *refs[9:11]), Along(grid.y, *refs[11:13])

    def drain(self):
        self.copies.drain()
        for one in (self.az, self.ax, self.ay):
            one.drain()

    def run(self):
        g = self.g
        across = self.copies.send(g.sibling, self.own, self.rc)
        yield
        across.wait_recv()
        self.pair[...] = self.own[...] + self.rc[...]
        self.az.start(lambda to: self.pair, lambda i: self.rz.at[i])
        yield
        self.az.wait()
        self.full[g.y.me, g.x.me] = self.pair[...] + jnp.sum(self.rz[...], axis=0)
        own, row = self.full.at[g.y.me, g.x.me], self.full.at[g.y.me]
        self.ax.start(lambda to: own, lambda i: own)
        yield
        self.ax.wait()
        self.ay.start(lambda to: row, lambda i: row)
        yield
        self.ay.wait()


class ExSum:
    @staticmethod
    def shape(nz, ranks, dims):
        r = max(8, ranks // nz)
        groups = ranks // r
        across = nz // groups
        return groups, across, r, dims // 2 // across

    @staticmethod
    def scratch(nz, ranks, dims):
        groups, across, r, w = ExSum.shape(nz, ranks, dims)
        blocks = (groups, across, r, w)
        return [
            pltpu.VMEM((2,) + blocks, F32),
            pltpu.VMEM(blocks, F32),
            pltpu.VMEM(blocks, F32),
            pltpu.VMEM((nz - 1, r, w), F32),
            pltpu.VMEM((2,) + blocks, F32),
        ] + Copies.scratch(2) + Along.scratch(nz) + Along.scratch(nz)

    def __init__(self, grid, refs):
        self.g = grid
        self.part, self.rc, self.pair, self.rz, self.full = refs[:5]
        self.copies = Copies(*refs[5:7])
        self.out, self.back = Along(grid.z, *refs[7:9]), Along(grid.z, *refs[9:11])

    def drain(self):
        self.copies.drain()
        self.out.drain()
        self.back.drain()

    def put(self, side, value):
        _, groups, across, r, w = self.part.shape
        for j in range(across):
            self.part[side, :, j] = value[:, j * w : (j + 1) * w].reshape(groups, r, w)

    def get(self, side):
        _, groups, across, r, w = self.part.shape
        return jnp.concatenate([self.full[side, :, j].reshape(groups * r, w) for j in range(across)], axis=1)

    def start(self):
        self.c0 = self.copies.send(self.g.sibling, self.part.at[1 - self.g.core], self.rc)

    def run(self):
        z, core = self.g.z, self.g.core
        across = self.part.shape[2]
        place = lambda i: (lax.div(i, across), lax.rem(i, across))
        self.c0.wait_recv()
        self.pair[...] = self.part[core] + self.rc[...]
        self.out.start(lambda to: self.pair.at[place(to)], lambda i: self.rz.at[i])
        yield
        self.out.wait()
        me = place(z.me)
        self.full[(core,) + me] = self.pair[me] + jnp.sum(self.rz[...], axis=0)
        own = self.full.at[(core,) + me]
        self.back.start(lambda to: own, lambda i: own)
        yield
        self.back.wait()
        half = self.full.at[core]
        c1 = self.copies.send(self.g.sibling, half, half)
        yield
        c1.wait_recv()


def kernel(nx, ny, nz, a_hbm, t_hbm, first_hbm, basis_hbm, proj_hbm, a_ref, t_ref, work, lhs_ref, terms_ref, turned_ref,
           inv0, inv1, first_ref, basis_ref, proj_ref, a_sem, t_sem, out_sem, *refs):
    g = Grid(nx, ny, nz)
    rows, dims = a_ref.shape
    h = dims // 2
    gr = RANK // (nx * ny)
    ranks = RANK // CHUNKS
    refs = list(refs)

    def take(kind, *sizes):
        n = len(kind.scratch(*sizes))
        out = kind(g, refs[:n])
        del refs[:n]
        return out

    feats, grams, exs = [], [], []
    for _ in range(2):
        feats.append([take(FeatSum, nx, ny, ranks, rows) for _ in range(CHUNKS)])
        grams.append(take(GramSum, nx, ny, nz))
        exs.append([take(ExSum, nz, ranks, dims) for _ in range(CHUNKS)])

    load_t = pltpu.make_async_copy(t_hbm, t_ref, t_sem)
    load_t.start()
    load_a = pltpu.make_async_copy(a_hbm, a_ref, a_sem)
    load_a.start()
    greeted = g.greet()

    scale = jnp.sqrt(jnp.float32(ROWS))
    shrink = 1.0 / jnp.sqrt(jnp.float32(DIMS))
    invs, outs = (inv0, inv1), ((first_ref, first_hbm), (basis_ref, basis_hbm))
    e = rows // (nx * ny)
    places = [(y, x) for y in range(ny) for x in range(nx)]

    def turn(s):
        for n, at in enumerate(places):
            block = jnp.concatenate([feats[s][c].full[at] for c in range(CHUNKS)], axis=0)
            turned_ref[n * e : (n + 1) * e, :] = block.T

    def write_rows(s):
        ref, hbm = outs[s]
        ref[...] = scale * lax.dot_general(
            turned_ref[...], invs[s][...], (((1,), (1,)), ((), ())), preferred_element_type=F32, precision=HIGHEST
        )
        copy = pltpu.make_async_copy(ref, hbm, out_sem.at[s])
        copy.start()
        return copy

    def own_gram(s):
        terms = terms_ref[...]
        raw = lax.dot_general(terms, terms, (((1,), (1,)), ((), ())), preferred_element_type=F32)
        for c in range(CHUNKS):
            r0 = 2 * c * ranks
            some = raw[r0 : r0 + ranks] + raw[r0 + ranks : r0 + 2 * ranks]
            parts = []
            for d in range(CHUNKS):
                c0 = 2 * d * ranks
                parts.append(some[:, c0 : c0 + ranks] + some[:, c0 + ranks : c0 + 2 * ranks])
            work[c * ranks : (c + 1) * ranks, 0:RANK] = jnp.concatenate(parts, axis=1)
        at = pl.ds(pl.multiple_of((g.y.me * nx + g.x.me) * gr, gr), gr)
        grams[s].own[...] = work[at, 0:RANK]

    def chain(s, c):
        feat, ex = feats[s][c], exs[s][c]
        prod = lax.dot_general(
            lhs_ref[c * ranks : (c + 1) * ranks, :], a_ref[...], (((1,), (1,)), ((), ())), preferred_element_type=F32
        )
        for n, at in enumerate(places):
            feat.part[at] = prod[:, n * e : (n + 1) * e]
        if s == 0 and c == 0:
            greeted()
        yield from feat.run()
        for n, at in enumerate(places):
            high, low = split(feat.full[at])
            terms_ref[2 * c * ranks : (2 * c + 1) * ranks, n * e : (n + 1) * e] = high
            terms_ref[(2 * c + 1) * ranks : (2 * c + 2) * ranks, n * e : (n + 1) * e] = low
        yield
        for n in range(2):
            side = 1 - g.core if n == 0 else g.core
            at = pl.ds(pl.multiple_of(side * h, h), h)
            prod = jnp.dot(terms_ref[2 * c * ranks : (2 * c + 2) * ranks, :], a_ref[:, at], preferred_element_type=F32)
            ex.put(side, prod[:ranks] + prod[ranks:])
            if n == 0:
                ex.start()
        yield
        yield from ex.run()

    def applied(s, c, side):
        out = 0.0
        for d in range(c + 1):
            inv = invs[s][c * ranks : (c + 1) * ranks, d * ranks : (d + 1) * ranks]
            out += jnp.dot(inv, exs[s][d].get(side), preferred_element_type=F32, precision=HIGHEST)
        return out

    load_t.wait()
    lhs_ref[...] = t_ref[...].astype(F32).T.astype(BF16)
    load_a.wait()
    chains = [chain(0, c) for c in range(CHUNKS)]
    for one in chains:
        next(one)
    for s in range(2):
        for _ in range(3):
            for one in chains:
                next(one)
        gram = grams[s].run()
        for c, one in enumerate(chains):
            next(one)
            if c == CHUNKS - 1:
                own_gram(s)
                next(gram)
            next(one)
            if c == CHUNKS - 1:
                next(gram)
            next(one)
        turn(s)
        next(chains[0])
        next(gram)
        for one in chains[1:]:
            next(one)
        next(gram)
        next(gram, None)
        work[:, 0:RANK] = grams[s].full[...].reshape(RANK, RANK)
        row = lax.broadcasted_iota(jnp.int32, (RANK, RANK), 0)
        column = lax.broadcasted_iota(jnp.int32, (RANK, RANK), 1)
        work[:, RANK : 2 * RANK] = jnp.where(row == column, 1.0, 0.0).astype(F32)
        panels = RANK // BLOCK
        factor(work, 0, panels // 2)
        if CHUNKS > 1:
            next(chains[0])
        factor(work, panels // 2, panels)
        invs[s][...] = work[:, RANK : 2 * RANK]
        if s == 1:
            out1 = write_rows(1)
        if CHUNKS == 1:
            next(chains[0])
        later = []
        for c in range(CHUNKS):
            if c > 0:
                next(chains[c])
            for n in range(2):
                side = g.core if n == 0 else 1 - g.core
                at = pl.ds(pl.multiple_of(side * h, h), h)
                if n == 1:
                    next(chains[c], None)
                if s == 0:
                    lhs_ref[c * ranks : (c + 1) * ranks, at] = (applied(s, c, side) * shrink).astype(BF16)
                else:
                    proj_ref[c * ranks : (c + 1) * ranks, at] = applied(s, c, side)
            if s == 0:
                later.append(chain(1, c))
                next(later[c])
        if s == 0:
            out0 = write_rows(0)
            chains = later
    out2 = pltpu.make_async_copy(proj_ref, proj_hbm, out_sem.at[2])
    out2.start()
    for s in range(2):
        for one in feats[s] + [grams[s]] + exs[s]:
            one.drain()
    out0.wait()
    out1.wait()
    out2.wait()


def shards(nx, ny, nz, features, test_matrix):
    rows, dims = features.shape
    ranks = RANK // CHUNKS
    hbm = pl.BlockSpec(memory_space=pl.ANY)
    scratch = [
        pltpu.VMEM((rows, dims), BF16),
        pltpu.VMEM((dims, RANK), BF16),
        pltpu.VMEM((RANK, 2 * RANK), F32),
        pltpu.VMEM((RANK, dims), BF16),
        pltpu.VMEM((2 * RANK, rows), BF16),
        pltpu.VMEM((rows, RANK), F32),
        pltpu.VMEM((RANK, RANK), F32),
        pltpu.VMEM((RANK, RANK), F32),
        pltpu.VMEM((rows, RANK), F32),
        pltpu.VMEM((rows, RANK), F32),
        pltpu.VMEM((RANK, dims), F32),
        pltpu.SemaphoreType.DMA,
        pltpu.SemaphoreType.DMA,
        pltpu.SemaphoreType.DMA((3,)),
    ]
    for _ in range(2):
        scratch += FeatSum.scratch(nx, ny, ranks, rows) * CHUNKS
        scratch += GramSum.scratch(nx, ny, nz)
        scratch += ExSum.scratch(nz, ranks, dims) * CHUNKS
    return pl.pallas_call(
        functools.partial(kernel, nx, ny, nz),
        out_shape=(
            jax.ShapeDtypeStruct((rows, RANK), F32),
            jax.ShapeDtypeStruct((rows, RANK), F32),
            jax.ShapeDtypeStruct((RANK, dims), F32),
        ),
        in_specs=[hbm, hbm],
        out_specs=(hbm, hbm, hbm),
        scratch_shapes=scratch,
        compiler_params=pltpu.CompilerParams(
            collective_id=0, has_side_effects=True, vmem_limit_bytes=48 * 1024 * 1024
        ),
        cost_estimate=pl.CostEstimate(flops=6 * rows * dims * RANK * 2, bytes_accessed=8 << 20, transcendentals=256),
    )(features, test_matrix)


def solution(mesh):
    feat, ex = mesh.shape["feat"], mesh.shape["ex"]
    nx = 4
    return jax.shard_map(
        functools.partial(shards, nx, feat // nx, ex // 2),
        mesh=mesh,
        in_specs=(P("ex", "feat"), P("feat", None)),
        out_specs=(P("ex", None), P("ex", None), P(None, "feat")),
        check_vma=False,
    )
```

```python
import functools

import jax
import jax.numpy as jnp
from jax import lax
from jax.experimental import pallas as pl
from jax.experimental.pallas import tpu as pltpu
from jax.sharding import PartitionSpec as P

DIMS = 16384
ROWS = 65536
RANK = 128
MESH = pl.DeviceIdType.MESH
F32 = jnp.float32
BF16 = jnp.bfloat16
HIGHEST = lax.Precision.HIGHEST
BLOCK = 8
EARLY = 4
CHUNKS = 2


def split(value):
    high = value.astype(BF16)
    return high, (value - high.astype(F32)).astype(BF16)


def factor(work, begin, end):
    lane = lax.broadcasted_iota(jnp.int32, (BLOCK, RANK), 1)

    def step(b, carry):
        at = pl.ds(pl.multiple_of(b * BLOCK, BLOCK), BLOCK)
        left = work[at, 0:RANK]
        right = work[at, RANK : 2 * RANK]
        diag = {}
        for j in range(BLOCK):
            column = jnp.sum(jnp.where(lane == b * BLOCK + j, left, 0.0), axis=1, keepdims=True)
            column = jnp.broadcast_to(column, (BLOCK, RANK))
            for i in range(j, BLOCK):
                diag[i, j] = column[i : i + 1, :]
        lrows = [left[i : i + 1, :] for i in range(BLOCK)]
        rrows = [right[i : i + 1, :] for i in range(BLOCK)]
        for j in range(BLOCK):
            inv = lax.rsqrt(diag[j, j])
            lrows[j] = lrows[j] * inv
            rrows[j] = rrows[j] * inv
            low = {i: diag[i, j] * inv for i in range(j + 1, BLOCK)}
            for i in range(j + 1, BLOCK):
                for k in range(j + 1, i + 1):
                    diag[i, k] = diag[i, k] - low[i] * low[k]
                lrows[i] = lrows[i] - low[i] * lrows[j]
                rrows[i] = rrows[i] - low[i] * rrows[j]
        left = jnp.concatenate(lrows, axis=0)
        right = jnp.concatenate(rrows, axis=0)
        below = jnp.where(lane >= (b + 1) * BLOCK, left, 0.0)
        both = jnp.concatenate([left, right], axis=1)
        work[...] -= lax.dot_general(
            below, both, (((0,), (0,)), ((), ())), preferred_element_type=F32, precision=HIGHEST
        )
        work[at, 0:RANK] = left
        work[at, RANK : 2 * RANK] = right
        return carry

    lax.fori_loop(begin, end, step, 0)


class Axis:
    def __init__(self, n, me, device):
        self.n, self.me, self.device = n, me, device

    def at(self, offset):
        return lax.rem(self.me + offset + self.n, self.n)

    def peer(self, offset):
        return self.device(self.at(offset))


class Grid:
    def __init__(self, nx, ny, nz):
        ex, feat = lax.axis_index("ex"), lax.axis_index("feat")
        x, y = lax.rem(feat, nx), lax.div(feat, nx)
        core, z = lax.rem(ex, 2), lax.div(ex, 2)
        self.core = core
        self.x = Axis(nx, x, lambda i: (ex, y * nx + i))
        self.y = Axis(ny, y, lambda i: (ex, i * nx + x))
        self.z = Axis(nz, z, lambda i: (i * 2 + core, feat))
        self.sibling = (z * 2 + 1 - core, feat)

    def greet(self):
        barrier = pltpu.get_barrier_semaphore()
        partners = [self.sibling]
        for axis in (self.x, self.y):
            partners += [axis.peer(k) for k in range(1, axis.n)]
        partners += [self.z.peer(k) for k in range(1, self.z.n)]
        for device in partners:
            pl.semaphore_signal(barrier, inc=1, device_id=device, device_id_type=MESH)
        return lambda: pl.semaphore_wait(barrier, len(partners))


class Copies:
    def __init__(self, send, recv):
        self.send_sem, self.recv_sem = send, recv
        self.started = []

    @staticmethod
    def scratch(n):
        return [pltpu.SemaphoreType.DMA((n,)), pltpu.SemaphoreType.DMA((n,))]

    def send(self, device, src, dst):
        n = len(self.started)
        copy = pltpu.make_async_remote_copy(
            src_ref=src, dst_ref=dst, send_sem=self.send_sem.at[n], recv_sem=self.recv_sem.at[n],
            device_id=device, device_id_type=MESH,
        )
        copy.start()
        self.started.append(copy)
        return copy

    def drain(self):
        for copy in self.started:
            copy.wait_send()


def far_first(axis, i):
    return lax.rem((2 * lax.rem(i, 2) - 1) * (axis.n // 2 - lax.div(i + 1, 2)) + axis.n, axis.n)


class Along:
    def __init__(self, axis, send, recv):
        self.axis, self.send_sem, self.recv_sem = axis, send, recv

    @staticmethod
    def scratch(n):
        return [pltpu.SemaphoreType.DMA((n - 1,)), pltpu.SemaphoreType.DMA((n - 1,))]

    def copy(self, i):
        to = self.axis.at(far_first(self.axis, i))
        return pltpu.make_async_remote_copy(
            src_ref=self.src(to), dst_ref=self.dst(i), send_sem=self.send_sem.at[i], recv_sem=self.recv_sem.at[i],
            device_id=self.axis.device(to), device_id_type=MESH,
        )

    def loop(self, act):
        def body(i, carry):
            act(self.copy(i))
            return carry

        if self.axis.n > 4:
            lax.fori_loop(0, self.axis.n - 1, body, 0)
        else:
            for i in range(self.axis.n - 1):
                body(i, 0)

    def start(self, src, dst):
        self.src, self.dst = src, dst
        self.loop(lambda copy: copy.start())

    def wait(self):
        self.loop(lambda copy: copy.wait_recv())

    def drain(self):
        self.loop(lambda copy: copy.wait_send())


class FeatSum:
    @staticmethod
    def scratch(nx, ny, ranks, rows):
        e, h = rows // (nx * ny), ranks // 2
        sems = []
        for _ in range(4):
            sems += Along.scratch(nx) + Along.scratch(ny)
        return [
            pltpu.VMEM((ny, nx, ranks, e), F32),
            pltpu.VMEM((ny, nx, ranks, e), F32),
            pltpu.VMEM((nx - 1, ny, h, e), F32),
            pltpu.VMEM((ny - 1, nx, h, e), F32),
            pltpu.VMEM((ny, h, e), F32),
            pltpu.VMEM((nx, h, e), F32),
            pltpu.VMEM((ny - 1, h, e), F32),
            pltpu.VMEM((nx - 1, h, e), F32),
        ] + sems

    def __init__(self, grid, refs):
        self.g = grid
        self.part, self.full, self.r1a, self.r1b, self.sa, self.sb, self.r2a, self.r2b = refs[:8]
        sems = refs[8:]
        self.ax = [Along(grid.x, *sems[4 * n : 4 * n + 2]) for n in range(4)]
        self.ay = [Along(grid.y, *sems[4 * n + 2 : 4 * n + 4]) for n in range(4)]

    def drain(self):
        for one in self.ax + self.ay:
            one.drain()

    def run(self):
        x, y = self.g.x, self.g.y
        part, full = self.part, self.full
        h = part.shape[2] // 2
        a, b = pl.ds(0, h), pl.ds(h, h)
        self.ax[0].start(lambda to: part.at[:, to, a], lambda i: self.r1a.at[i])
        self.ay[0].start(lambda to: part.at[to, :, b], lambda i: self.r1b.at[i])
        yield
        self.ax[0].wait()
        self.sa[...] = part[:, x.me, a] + sum(self.r1a[i] for i in range(x.n - 1))
        self.ay[1].start(lambda to: self.sa.at[to], lambda i: self.r2a.at[i])
        self.ay[0].wait()
        self.sb[...] = part[y.me, :, b] + sum(self.r1b[i] for i in range(y.n - 1))
        self.ax[1].start(lambda to: self.sb.at[to], lambda i: self.r2b.at[i])
        yield
        own_a, own_b = full.at[y.me, x.me, a], full.at[y.me, x.me, b]
        self.ay[1].wait()
        own_a[...] = self.sa[y.me] + sum(self.r2a[i] for i in range(y.n - 1))
        self.ay[2].start(lambda to: own_a, lambda i: own_a)
        self.ax[1].wait()
        own_b[...] = self.sb[x.me] + sum(self.r2b[i] for i in range(x.n - 1))
        self.ax[2].start(lambda to: own_b, lambda i: own_b)
        yield
        column_a, row_b = full.at[:, x.me, a], full.at[y.me, :, b]
        self.ay[2].wait()
        self.ax[3].start(lambda to: column_a, lambda i: column_a)
        self.ax[2].wait()
        self.ay[3].start(lambda to: row_b, lambda i: row_b)
        yield
        self.ax[3].wait()
        self.ay[3].wait()


class GramSum:
    @staticmethod
    def scratch(nx, ny, nz):
        r = RANK // (nx * ny) // 2
        return [
            pltpu.VMEM((2, r, RANK), F32),
            pltpu.VMEM((r, RANK), F32),
            pltpu.VMEM((r, RANK), F32),
            pltpu.VMEM((nz - 1, r, RANK), F32),
            pltpu.VMEM((ny, nx, 2, r, RANK), F32),
        ] + Copies.scratch(2) + Along.scratch(nz) + Along.scratch(nx) + Along.scratch(ny)

    def __init__(self, grid, refs):
        self.g = grid
        self.own, self.rc, self.pair, self.rz, self.full = refs[:5]
        self.copies = Copies(*refs[5:7])
        self.az, self.ax, self.ay = Along(grid.z, *refs[7:9]), Along(grid.x, *refs[9:11]), Along(grid.y, *refs[11:13])

    def drain(self):
        self.copies.drain()
        for one in (self.az, self.ax, self.ay):
            one.drain()

    def run(self):
        g = self.g
        across = self.copies.send(g.sibling, self.own.at[1 - g.core], self.rc)
        yield
        across.wait_recv()
        self.pair[...] = self.own[g.core] + self.rc[...]
        self.az.start(lambda to: self.pair, lambda i: self.rz.at[i])
        yield
        self.az.wait()
        mine = self.full.at[g.y.me, g.x.me, g.core]
        mine[...] = self.pair[...] + jnp.sum(self.rz[...], axis=0)
        across = self.copies.send(g.sibling, mine, mine)
        across.wait_recv()
        own, row = self.full.at[g.y.me, g.x.me], self.full.at[g.y.me]
        self.ax.start(lambda to: own, lambda i: own)
        yield
        self.ax.wait()
        self.ay.start(lambda to: row, lambda i: row)
        yield
        self.ay.wait()


class ExSum:
    @staticmethod
    def shape(nz, ranks, dims):
        r = max(8, ranks // nz)
        groups = ranks // r
        across = nz // groups
        return groups, across, r, dims // 2 // across

    @staticmethod
    def scratch(nz, ranks, dims):
        groups, across, r, w = ExSum.shape(nz, ranks, dims)
        blocks = (groups, across, r, w)
        return [
            pltpu.VMEM((2,) + blocks, F32),
            pltpu.VMEM(blocks, F32),
            pltpu.VMEM(blocks, F32),
            pltpu.VMEM((nz - 1, r, w), F32),
            pltpu.VMEM((2,) + blocks, F32),
        ] + Copies.scratch(2) + Along.scratch(nz) + Along.scratch(nz)

    def __init__(self, grid, refs):
        self.g = grid
        self.part, self.rc, self.pair, self.rz, self.full = refs[:5]
        self.copies = Copies(*refs[5:7])
        self.out, self.back = Along(grid.z, *refs[7:9]), Along(grid.z, *refs[9:11])

    def drain(self):
        self.copies.drain()
        self.out.drain()
        self.back.drain()

    def put(self, side, value):
        _, groups, across, r, w = self.part.shape
        for j in range(across):
            self.part[side, :, j] = value[:, j * w : (j + 1) * w].reshape(groups, r, w)

    def get(self, side):
        _, groups, across, r, w = self.part.shape
        return jnp.concatenate([self.full[side, :, j].reshape(groups * r, w) for j in range(across)], axis=1)

    def start(self):
        self.c0 = self.copies.send(self.g.sibling, self.part.at[1 - self.g.core], self.rc)

    def run(self):
        z, core = self.g.z, self.g.core
        across = self.part.shape[2]
        place = lambda i: (lax.div(i, across), lax.rem(i, across))
        self.c0.wait_recv()
        self.pair[...] = self.part[core] + self.rc[...]
        self.out.start(lambda to: self.pair.at[place(to)], lambda i: self.rz.at[i])
        yield
        self.out.wait()
        me = place(z.me)
        self.full[(core,) + me] = self.pair[me] + jnp.sum(self.rz[...], axis=0)
        own = self.full.at[(core,) + me]
        self.back.start(lambda to: own, lambda i: own)
        yield
        self.back.wait()
        half = self.full.at[core]
        c1 = self.copies.send(self.g.sibling, half, half)
        yield
        c1.wait_recv()


def kernel(nx, ny, nz, a_hbm, t_hbm, first_hbm, basis_hbm, proj_hbm, a_ref, t_ref, work, lhs_ref, terms_ref, turned_ref,
           inv0, inv1, first_ref, basis_ref, proj_ref, a_sem, t_sem, out_sem, *refs):
    g = Grid(nx, ny, nz)
    rows, dims = a_ref.shape
    h = dims // 2
    gr = RANK // (nx * ny)
    ranks = RANK // CHUNKS
    refs = list(refs)

    def take(kind, *sizes):
        n = len(kind.scratch(*sizes))
        out = kind(g, refs[:n])
        del refs[:n]
        return out

    feats, grams, exs = [], [], []
    for _ in range(2):
        feats.append([take(FeatSum, nx, ny, ranks, rows) for _ in range(CHUNKS)])
        grams.append(take(GramSum, nx, ny, nz))
        exs.append([take(ExSum, nz, ranks, dims) for _ in range(CHUNKS)])

    load_t = pltpu.make_async_copy(t_hbm, t_ref, t_sem)
    load_t.start()
    load_a = pltpu.make_async_copy(a_hbm, a_ref, a_sem)
    load_a.start()
    greeted = g.greet()

    scale = jnp.sqrt(jnp.float32(ROWS))
    shrink = 1.0 / jnp.sqrt(jnp.float32(DIMS))
    invs, outs = (inv0, inv1), ((first_ref, first_hbm), (basis_ref, basis_hbm))
    e = rows // (nx * ny)
    places = [(y, x) for y in range(ny) for x in range(nx)]

    def turn(s):
        for n, at in enumerate(places):
            block = jnp.concatenate([feats[s][c].full[at] for c in range(CHUNKS)], axis=0)
            turned_ref[n * e : (n + 1) * e, :] = block.T

    def write_rows(s):
        ref, hbm = outs[s]
        ref[...] = scale * lax.dot_general(
            turned_ref[...], invs[s][...], (((1,), (1,)), ((), ())), preferred_element_type=F32, precision=HIGHEST
        )
        copy = pltpu.make_async_copy(ref, hbm, out_sem.at[s])
        copy.start()
        return copy

    def own_gram(s):
        terms = terms_ref[...]
        raw = lax.dot_general(terms, terms, (((1,), (1,)), ((), ())), preferred_element_type=F32)
        for c in range(CHUNKS):
            r0 = 2 * c * ranks
            some = raw[r0 : r0 + ranks] + raw[r0 + ranks : r0 + 2 * ranks]
            parts = []
            for d in range(CHUNKS):
                c0 = 2 * d * ranks
                parts.append(some[:, c0 : c0 + ranks] + some[:, c0 + ranks : c0 + 2 * ranks])
            work[c * ranks : (c + 1) * ranks, 0:RANK] = jnp.concatenate(parts, axis=1)
        at = pl.ds(pl.multiple_of((g.y.me * nx + g.x.me) * gr, gr), gr)
        own = work[at, 0:RANK]
        for n in range(2):
            grams[s].own[n] = own[n * (gr // 2) : (n + 1) * (gr // 2)]

    def chain(s, c):
        feat, ex = feats[s][c], exs[s][c]
        prod = lax.dot_general(
            lhs_ref[c * ranks : (c + 1) * ranks, :], a_ref[...], (((1,), (1,)), ((), ())), preferred_element_type=F32
        )
        for n, at in enumerate(places):
            feat.part[at] = prod[:, n * e : (n + 1) * e]
        if s == 0 and c == 0:
            greeted()
        yield from feat.run()
        for n, at in enumerate(places):
            high, low = split(feat.full[at])
            terms_ref[2 * c * ranks : (2 * c + 1) * ranks, n * e : (n + 1) * e] = high
            terms_ref[(2 * c + 1) * ranks : (2 * c + 2) * ranks, n * e : (n + 1) * e] = low
        yield
        for n in range(2):
            side = 1 - g.core if n == 0 else g.core
            at = pl.ds(pl.multiple_of(side * h, h), h)
            prod = jnp.dot(terms_ref[2 * c * ranks : (2 * c + 2) * ranks, :], a_ref[:, at], preferred_element_type=F32)
            ex.put(side, prod[:ranks] + prod[ranks:])
            if n == 0:
                ex.start()
            yield
        yield from ex.run()

    def applied(s, c, side):
        out = 0.0
        for d in range(c + 1):
            inv = invs[s][c * ranks : (c + 1) * ranks, d * ranks : (d + 1) * ranks]
            out += jnp.dot(inv, exs[s][d].get(side), preferred_element_type=F32, precision=HIGHEST)
        return out

    load_t.wait()
    lhs_ref[...] = t_ref[...].astype(F32).T.astype(BF16)
    load_a.wait()
    chains = [chain(0, c) for c in range(CHUNKS)]
    for one in chains:
        next(one)
    for s in range(2):
        for _ in range(3):
            for one in chains:
                next(one)
        gram = grams[s].run()
        for one in chains:
            next(one)
        own_gram(s)
        next(gram)
        for c, one in enumerate(chains):
            next(one)
            if c == 0:
                next(gram)
            next(one)
            next(one)
        next(gram)
        turn(s)
        next(gram)
        next(chains[0])
        next(gram, None)
        for n, (y, x) in enumerate(places):
            for half in range(2):
                begin = n * gr + half * (gr // 2)
                work[begin : begin + gr // 2, 0:RANK] = grams[s].full[y, x, half]
        row = lax.broadcasted_iota(jnp.int32, (RANK, RANK), 0)
        column = lax.broadcasted_iota(jnp.int32, (RANK, RANK), 1)
        work[:, RANK : 2 * RANK] = jnp.where(row == column, 1.0, 0.0).astype(F32)
        panels = RANK // BLOCK
        factor(work, 0, EARLY)
        for one in chains[1:]:
            next(one)
        factor(work, EARLY, panels)
        invs[s][...] = work[:, RANK : 2 * RANK]
        if s == 1:
            out1 = write_rows(1)
        later = []
        for c in range(CHUNKS):
            next(chains[c])
            for n in range(2):
                side = g.core if n == 0 else 1 - g.core
                at = pl.ds(pl.multiple_of(side * h, h), h)
                if n == 1:
                    next(chains[c], None)
                if s == 0:
                    lhs_ref[c * ranks : (c + 1) * ranks, at] = (applied(s, c, side) * shrink).astype(BF16)
                else:
                    proj_ref[c * ranks : (c + 1) * ranks, at] = applied(s, c, side)
            if s == 0:
                later.append(chain(1, c))
                next(later[c])
        if s == 0:
            out0 = write_rows(0)
            chains = later
    out2 = pltpu.make_async_copy(proj_ref, proj_hbm, out_sem.at[2])
    out2.start()
    for s in range(2):
        for one in feats[s] + [grams[s]] + exs[s]:
            one.drain()
    out0.wait()
    out1.wait()
    out2.wait()


def shards(nx, ny, nz, features, test_matrix):
    rows, dims = features.shape
    ranks = RANK // CHUNKS
    hbm = pl.BlockSpec(memory_space=pl.ANY)
    scratch = [
        pltpu.VMEM((rows, dims), BF16),
        pltpu.VMEM((dims, RANK), BF16),
        pltpu.VMEM((RANK, 2 * RANK), F32),
        pltpu.VMEM((RANK, dims), BF16),
        pltpu.VMEM((2 * RANK, rows), BF16),
        pltpu.VMEM((rows, RANK), F32),
        pltpu.VMEM((RANK, RANK), F32),
        pltpu.VMEM((RANK, RANK), F32),
        pltpu.VMEM((rows, RANK), F32),
        pltpu.VMEM((rows, RANK), F32),
        pltpu.VMEM((RANK, dims), F32),
        pltpu.SemaphoreType.DMA,
        pltpu.SemaphoreType.DMA,
        pltpu.SemaphoreType.DMA((3,)),
    ]
    for _ in range(2):
        scratch += FeatSum.scratch(nx, ny, ranks, rows) * CHUNKS
        scratch += GramSum.scratch(nx, ny, nz)
        scratch += ExSum.scratch(nz, ranks, dims) * CHUNKS
    return pl.pallas_call(
        functools.partial(kernel, nx, ny, nz),
        out_shape=(
            jax.ShapeDtypeStruct((rows, RANK), F32),
            jax.ShapeDtypeStruct((rows, RANK), F32),
            jax.ShapeDtypeStruct((RANK, dims), F32),
        ),
        in_specs=[hbm, hbm],
        out_specs=(hbm, hbm, hbm),
        scratch_shapes=scratch,
        compiler_params=pltpu.CompilerParams(
            collective_id=0, has_side_effects=True, vmem_limit_bytes=48 * 1024 * 1024
        ),
        cost_estimate=pl.CostEstimate(flops=6 * rows * dims * RANK * 2, bytes_accessed=8 << 20, transcendentals=256),
    )(features, test_matrix)


def solution(mesh):
    feat, ex = mesh.shape["feat"], mesh.shape["ex"]
    nx = 4
    return jax.shard_map(
        functools.partial(shards, nx, feat // nx, ex // 2),
        mesh=mesh,
        in_specs=(P("ex", "feat"), P("feat", None)),
        out_specs=(P("ex", None), P("ex", None), P(None, "feat")),
        check_vma=False,
    )
```
